32 devices in a mesh: row: 8 (over y, x, core), col: 4 (over z).
Axes of the slice: x: 2, y: 2, z: 4, core: 2. Of those that a mesh axis runs over, the one named last changes fastest.
Arguments:
- band_cells: float32 [3, 256, 2], P(None, ('row', 'col')), may hold values from 0 to 1
- cell_counts: int32 [256], P(('row', 'col')), may hold values from 1 to 2, as said below
- cell_assign: int32 [256], P(('row', 'col')), may hold values from 0 to 255, as said below
- wake_pos: float32 [3, 262144], P(None, ('row', 'col')), may hold values from 0 to 1
- wake_strength: float32 [3, 262144], P(None, ('row', 'col')), may hold values from -0.01171875 to 0.01171875
- wake_core: float32 [1, 262144], P(None, ('row', 'col')), may hold values from 0.05 to 0.15
Outputs:
- velocity: float32 [3, 256, 2], P(None, ('row', 'col'))
- gradient: float32 [9, 256, 2], P(None, ('row', 'col'))
The draws below stay inside these ranges and needn't reach their ends.
Inputs may be any that keep to these rules, and one draw needn't show every extreme that they name: `cell_counts`: each band cell holds its live particles in its first slots; some cell is full in every draw. `cell_assign`: A permutation of the cells. The cells of the device with index d along row+col go to positions q with q // 32 == d // 4; at most 2 of them land in the positions of any one device (q // 8); where 8 is a multiple of 4, exactly 2 land in the positions of each device of the group, else some pair of devices reaches 2.
All inputs are finite; a program needn't handle non-finite values.
Results may differ from the reference program's by a relative error of at most 0.0003.
Values sent between devices are 32-bit elements; how exact they have to be, the bound alone decides.
A program may use at most 64 MiB of HBM per device.

```python
import math
import jax
import jax.numpy as jnp
from jax import lax

CAP = 2
TILE_DEV = 8
GROUP_DEVS = 4
ROW_DEVS = 8
CELLS = 256
SOURCES = 262144


def draw_cell_counts(key, part):
    values_drawn = jax.random.randint(key, (CELLS,), 1, CAP + 1)
    full_index = jax.random.randint(jax.random.fold_in(key, 1), (), 0, CELLS)
    return values_drawn.at[full_index].set(CAP).astype(jnp.int32)


def draw_cell_assign(key, part):
    cell_ids = jnp.arange(CELLS, dtype=jnp.int32)
    device_ids = cell_ids // TILE_DEV
    within = cell_ids % TILE_DEV
    group_ids = device_ids // GROUP_DEVS
    col_ids = device_ids % GROUP_DEVS
    offsets = jax.random.permutation(jax.random.fold_in(key, 11), GROUP_DEVS).astype(jnp.int32)
    relabel_in = jax.vmap(lambda sub: jax.random.permutation(sub, GROUP_DEVS))(jax.random.split(jax.random.fold_in(key, 12), ROW_DEVS)).astype(jnp.int32)
    relabel_out = jax.vmap(lambda sub: jax.random.permutation(sub, GROUP_DEVS))(jax.random.split(jax.random.fold_in(key, 13), ROW_DEVS)).astype(jnp.int32)
    slot_order = jax.vmap(lambda sub: jax.random.permutation(sub, TILE_DEV))(jax.random.split(jax.random.fold_in(key, 14), ROW_DEVS)).astype(jnp.int32)
    shifted = (relabel_in[group_ids, col_ids] + offsets[within % GROUP_DEVS]) % GROUP_DEVS
    target_dev = relabel_out[group_ids, shifted]
    return ((group_ids * GROUP_DEVS + target_dev) * TILE_DEV + slot_order[group_ids, within]).astype(jnp.int32)


def block_scale(key, extent, cuts, least, high):
    gain = 1.0
    for dim, parts in cuts:
        heights = jax.random.uniform(jax.random.fold_in(jax.random.fold_in(key, 6), dim), (parts,), jnp.float32, least / len(cuts), high / len(cuts))
        gain = gain * jnp.repeat(jnp.exp(heights), extent[dim] // parts).reshape((-1,) + (1,) * (len(extent) - 1 - dim))
    return gain


def gaussian(stream_key, dims, width, limit, shards=(), held_as=jnp.bfloat16):
    drawn = jax.random.normal(stream_key, dims, jnp.float32) * width
    if len(shards) > 0:
        drawn = block_scale(stream_key, dims, shards, -0.22, 0.18) * drawn
    return jnp.clip(drawn, min=-limit, max=limit).astype(held_as)


def setup_inputs(seed: int = 0) -> dict:
    streams_of = jax.random.split(jax.random.key(seed), 7)
    band_cells = jnp.clip(1.0 * jax.random.uniform(streams_of[0], (3, CELLS, CAP), jnp.float32) ** block_scale(streams_of[0], (3, CELLS, CAP), ((1, 32),), -0.2, 0.2), 0.0, 1.0)
    cell_counts = draw_cell_counts(jax.random.fold_in(streams_of[6], 71), 0)
    cell_assign = draw_cell_assign(jax.random.fold_in(streams_of[6], 71), 0)
    wake_pos = jnp.clip(1.0 * jax.random.uniform(streams_of[3], (3, SOURCES), jnp.float32) ** block_scale(streams_of[3], (3, SOURCES), ((1, 32),), -0.2, 0.2), 0.0, 1.0)
    wake_strength = gaussian(streams_of[4], (3, SOURCES), SOURCES ** -0.5, 0.01171875, ((1, 32),), jnp.float32)
    wake_core = jnp.clip(jnp.exp(math.log(0.15) - 1.0986123 * jax.random.uniform(streams_of[5], (1, SOURCES), jnp.float32) ** block_scale(streams_of[5], (1, SOURCES), ((1, 32),), -0.2, 0.2)), 0.05, 0.15)
    return dict(band_cells=band_cells, cell_counts=cell_counts, cell_assign=cell_assign, wake_pos=wake_pos, wake_strength=wake_strength, wake_core=wake_core)


def block_sums(target_pos, source_pos, source_str, source_core):
    delta_x = target_pos[0][:, None] - source_pos[0][None, :]
    delta_y = target_pos[1][:, None] - source_pos[1][None, :]
    delta_z = target_pos[2][:, None] - source_pos[2][None, :]
    radius_sq = delta_x * delta_x + delta_y * delta_y + delta_z * delta_z + source_core[0][None, :] * source_core[0][None, :]
    inverse = lax.rsqrt(radius_sq)
    kernel_three = inverse * inverse * inverse
    kernel_five = kernel_three * inverse * inverse
    alpha_x = source_str[0][None, :]
    alpha_y = source_str[1][None, :]
    alpha_z = source_str[2][None, :]
    cross_x = delta_y * alpha_z - delta_z * alpha_y
    cross_y = delta_z * alpha_x - delta_x * alpha_z
    cross_z = delta_x * alpha_y - delta_y * alpha_x
    terms_list = [kernel_three * cross_x, kernel_three * cross_y, kernel_three * cross_z, kernel_three * alpha_x, kernel_three * alpha_y, kernel_three * alpha_z]
    for along in (delta_x, delta_y, delta_z):
        for cross in (cross_x, cross_y, cross_z):
            terms_list.append(kernel_five * along * cross)
    return jnp.stack([lax.optimization_barrier(jnp.sum(term, axis=1)) for term in terms_list])

def pair_sums(target_pos, source_pos, source_str, source_core, block_width):
    block_steps = source_pos.shape[1] // block_width

    def one_block(running, block_index):
        offset = block_index * block_width
        part_pos = lax.dynamic_slice_in_dim(source_pos, offset, block_width, 1)
        part_str = lax.dynamic_slice_in_dim(source_str, offset, block_width, 1)
        part_core = lax.dynamic_slice_in_dim(source_core, offset, block_width, 1)
        return (running + block_sums(target_pos, part_pos, part_str, part_core), None)
    start_sums = jnp.zeros((15, target_pos.shape[1]), jnp.float32)
    running, unused = lax.scan(one_block, start_sums, jnp.arange(block_steps, dtype=jnp.int32))
    return running

def finish(kernel_sums, slot_counts, slot_cap):
    biot_scale = -1.0 / (4.0 * math.pi)
    swirl_x, swirl_y, swirl_z = (kernel_sums[3], kernel_sums[4], kernel_sums[5])
    zero_row = jnp.zeros_like(swirl_x)
    levi_terms = [[zero_row, swirl_z, -swirl_y], [-swirl_z, zero_row, swirl_x], [swirl_y, -swirl_x, zero_row]]
    grad_rows = []
    for comp_m in range(3):
        for comp_n in range(3):
            grad_rows.append(biot_scale * (levi_terms[comp_m][comp_n] - 3.0 * kernel_sums[6 + comp_n * 3 + comp_m]))
    slot_ids = jnp.arange(slot_cap).astype(slot_counts.dtype)
    alive_mask = (slot_ids[None, :] < slot_counts[:, None]).astype(jnp.float32).reshape(-1)
    velocity = biot_scale * kernel_sums[0:3] * alive_mask[None, :]
    gradient = jnp.stack(grad_rows) * alive_mask[None, :]
    cell_total = slot_counts.shape[0]
    return (velocity.reshape(3, cell_total, slot_cap), gradient.reshape(9, cell_total, slot_cap))

def reference(band_cells, cell_counts, cell_assign, wake_pos, wake_strength, wake_core):
    relaid_cells = jnp.zeros_like(band_cells).at[:, cell_assign, :].set(band_cells)
    relaid_counts = jnp.zeros_like(cell_counts).at[cell_assign].set(cell_counts)
    target_pos = relaid_cells.reshape(3, -1)
    block_width = math.gcd(wake_pos.shape[1], 4096)
    kernel_sums = pair_sums(target_pos, wake_pos, wake_strength, wake_core, block_width)
    return finish(kernel_sums, relaid_counts, band_cells.shape[2])
```

```python
import functools
import math

import jax
import jax.numpy as jnp
from jax import lax
from jax.experimental import pallas as pl
from jax.experimental.pallas import tpu as pltpu
from jax.sharding import PartitionSpec as P

MESH = pl.DeviceIdType.MESH
LANES = 128
SUB = 8
CHUNK = 512
PREPARE = 1024
ROWS = 512
STRIP = 32
DEPTH = 48
CENTRE = 0.5


def split_three(value):
    high = value.astype(jnp.bfloat16).astype(jnp.float32)
    rest = value - high
    middle = rest.astype(jnp.bfloat16).astype(jnp.float32)
    return high, middle, rest - middle


def kernel(
    grid_rows, grid_cols,
    band_hbm, counts_hbm, assign_hbm, pos_hbm, str_hbm, core_hbm,
    inbox,
    band_ref, counts_ref, assign_ref, pos_ref, str_ref, core_ref, fetch,
    even, odd, note, notes, turned, place, left, source, weights, sums, parcel, own,
    note_send, note_recv, parcel_send, parcel_recv,
):
    total = grid_rows * grid_cols
    slots, cells = band_ref.shape[1:]
    block = cells * grid_cols
    width = note.shape[2] // slots
    held = cells * slots
    targets = total * held
    me_row = lax.axis_index("row")
    me_col = lax.axis_index("col")
    me = me_row * grid_cols + me_col

    fetches = [
        pltpu.make_async_copy(far, near, fetch.at[i])
        for i, (far, near) in enumerate(
            [
                (assign_hbm, assign_ref), (band_hbm, band_ref), (counts_hbm, counts_ref),
                (pos_hbm, pos_ref), (str_hbm, str_ref), (core_hbm, core_ref),
            ]
        )
    ]
    for one in fetches:
        one.start()

    def each_other(act):
        others = [lax.rem(me_col + z, grid_cols) for z in range(grid_cols)]
        for z in range(1, grid_cols):
            act((me_row, others[z]), me_row * grid_cols + others[z])

        def in_row(step, unused):
            there = lax.rem(me_row + step, grid_rows)
            for z in range(grid_cols):
                act((there, others[z]), there * grid_cols + others[z])
            return unused

        lax.fori_loop(1, grid_rows, in_row, 0)

    barrier = pltpu.get_barrier_semaphore()

    def greet(there, other):
        pl.semaphore_signal(barrier, inc=1, device_id=there, device_id_type=MESH)

    each_other(greet)

    for one in fetches[:3]:
        one.wait()
    lane = lax.broadcasted_iota(jnp.int32, (cells, width), 1)
    row = lax.broadcasted_iota(jnp.int32, (cells, width), 0)
    position = jnp.zeros((cells, width), jnp.int32)
    live = jnp.zeros((cells, width), jnp.float32)
    columns = [[jnp.zeros((cells, width), jnp.float32)] * slots for k in range(3)]
    for t in range(cells):
        for k in range(3):
            for s in range(slots):
                columns[k][s] = jnp.where(row == t, band_ref[k, s, t], columns[k][s])
        position = jnp.where(row == t, lax.rem(assign_ref[t], block), position)
        live = jnp.where(row == t, counts_ref[t].astype(jnp.float32), live)
    chosen = lax.rem(lane, block) == position
    kind = lane // block
    for s in range(slots):
        value = jnp.where(kind == 3, live, 0.0)
        for k in range(3):
            value = jnp.where(kind == k, columns[k][s] - CENTRE, value)
        value = jnp.where(chosen, value, 0.0)
        note[0, :, s * width : (s + 1) * width] = jnp.sum(value, axis=0, keepdims=True)

    pl.semaphore_wait(barrier, total - 1)

    def tell(there, other):
        pltpu.make_async_remote_copy(
            src_ref=note.at[0], dst_ref=notes.at[me], send_sem=note_send, recv_sem=note_recv,
            device_id=there, device_id_type=MESH,
        ).start()

    each_other(tell)
    notes[me] = note[0]

    for one in fetches[3:]:
        one.wait()
    span = source.shape[1]

    def prepare(index, unused):
        cols = pl.ds(pl.multiple_of(index * PREPARE, PREPARE), PREPARE)
        ys = [pos_ref[k : k + 1, cols] - CENTRE for k in range(3)]
        al = [str_ref[k : k + 1, cols] for k in range(3)]
        core = core_ref[0:1, cols]
        core_sq = core * core
        norm = ys[0] * ys[0] + ys[1] * ys[1] + ys[2] * ys[2] + core_sq
        be = [
            ys[(m + 1) % 3] * al[(m + 2) % 3] - ys[(m + 2) % 3] * al[(m + 1) % 3]
            for m in range(3)
        ]
        ones = jnp.ones((1, PREPARE), jnp.float32)
        blank = jnp.zeros((3, PREPARE), jnp.float32)
        one, two, three = split_three(jnp.concatenate(ys + [norm, ones, blank], axis=0))
        source[:, cols] = jnp.concatenate([one, one, one, two, two, three], axis=0).astype(
            jnp.bfloat16
        )
        pad = jnp.zeros((2, PREPARE), jnp.float32)
        base = jnp.concatenate(al + be + [pad], axis=0)
        split = [split_three(base)] + [split_three(base * g) for g in ys + [norm]]
        rows = [split[b][j] for j in range(3) for b in range(5)]
        rows.append(jnp.zeros((SUB, PREPARE), jnp.float32))
        weights[:, cols] = jnp.concatenate(rows, axis=0).astype(jnp.bfloat16)
        return unused

    lax.fori_loop(0, span // PREPARE, prepare, 0)

    pltpu.make_async_copy(
        notes.at[pl.ds(0, total - 1)], notes.at[pl.ds(0, total - 1)], note_recv
    ).wait()
    turned[...] = jnp.zeros_like(turned)
    for g in range(grid_rows):
        merged = notes[g * grid_cols]
        for z in range(1, grid_cols):
            merged = merged + notes[g * grid_cols + z]
        for s in range(slots):
            turned[g * slots + s : g * slots + s + 1, :] = merged[:, s * width : (s + 1) * width]
    columns = jnp.concatenate(
        [turned[:, w : w + LANES].T for w in range(0, width, LANES)], axis=0
    )
    for g in range(grid_rows):
        for z in range(grid_cols):
            for s in range(slots):
                at = ((g * grid_cols + z) * slots + s) * cells
                for k in range(4):
                    low = k * block + z * cells
                    column = columns[low : low + cells, g * slots + s : g * slots + s + 1]
                    wide = jnp.broadcast_to(column, (cells, LANES))
                    if k == 3:
                        wide = jnp.where(wide > s + 0.5, 1.0, 0.0)
                    place[k, at : at + cells, :] = wide

    def sides(index, unused):
        rows = pl.ds(pl.multiple_of(index * LANES, LANES), LANES)
        lane = lax.broadcasted_iota(jnp.int32, (LANES, LANES), 1)
        xs = [place[k, rows, :] for k in range(3)]
        value = jnp.where(lane % SUB == 3, 1.0, 0.0)
        value = jnp.where(
            lane % SUB == 4, xs[0] * xs[0] + xs[1] * xs[1] + xs[2] * xs[2], value
        )
        for k in range(3):
            value = jnp.where(lane % SUB == k, -2.0 * xs[k], value)
        one, two, three = split_three(value)
        part = lane // SUB
        value = jnp.where((part == 1) | (part == 4), two, jnp.where(part == 2, three, one))
        left[rows, :] = jnp.where(part < 6, value, 0.0).astype(jnp.bfloat16)
        return unused

    lax.fori_loop(0, targets // LANES, sides, 0)

    sums[...] = jnp.zeros_like(sums)

    parts = targets // ROWS
    steps = (span // CHUNK) * parts

    def where_at(index):
        cols = pl.ds(pl.multiple_of((index // parts) * CHUNK, CHUNK), CHUNK)
        first = lax.rem(index, parts) * ROWS
        return cols, first

    def powers(index, store):
        cols, first = where_at(index)

        rows = pl.ds(pl.multiple_of(first, ROWS), ROWS)
        radius = jnp.dot(
            left[rows, 0:DEPTH], source[:, cols], preferred_element_type=jnp.float32
        )
        for low in range(0, ROWS, STRIP):
            inverse = lax.rsqrt(radius[low : low + STRIP])
            square = inverse * inverse
            power = square * square * inverse
            high = power.astype(jnp.bfloat16)
            rest = (power - high.astype(jnp.float32)).astype(jnp.bfloat16)
            store[low : low + STRIP, 0:CHUNK] = high
            store[low : low + STRIP, CHUNK : 2 * CHUNK] = rest

    def add(index, store):
        cols, first = where_at(index)
        rows = pl.ds(pl.multiple_of(first, ROWS), ROWS)
        both = jnp.concatenate([weights[:, cols]] * 2, axis=1)
        sums[rows, :] += lax.dot_general(
            store[...], both, (((1,), (1,)), ((), ())), preferred_element_type=jnp.float32
        )

    powers(0, even)

    def pairs(count, unused):
        index = 2 * count
        add(index, even)
        powers(index + 1, odd)
        add(index + 1, odd)
        powers(index + 2, even)
        return unused

    lax.fori_loop(0, steps // 2 - 1, pairs, 0)
    add(steps - 2, even)
    powers(steps - 1, odd)
    add(steps - 1, odd)

    scale = -1.0 / (4.0 * math.pi)
    lane = lax.broadcasted_iota(jnp.int32, (LANES, LANES), 1)
    sub = lax.broadcasted_iota(jnp.int32, (SUB, LANES), 0)
    group = lax.broadcasted_iota(jnp.int32, (SUB, LANES), 1) // held
    for i in range(targets // LANES):
        rows = slice(i * LANES, (i + 1) * LANES)
        tile = sums[rows, :]
        for k in range(4):
            tile = jnp.where(lane == 120 + k, place[k, rows, :], tile)
        tile = tile.T
        moment = [
            tile[b * SUB : (b + 1) * SUB]
            + (tile[40 + b * SUB : 48 + b * SUB] + tile[80 + b * SUB : 88 + b * SUB])
            for b in range(5)
        ]
        xs = [tile[120 + k : 121 + k] for k in range(3)]
        alive = tile[123:124]
        norm = xs[0] * xs[0] + xs[1] * xs[1] + xs[2] * xs[2]
        swirl = norm * moment[0] + moment[4]
        for n in range(3):
            swirl = swirl - (2.0 * xs[n]) * moment[1 + n]

        def cross(table):
            return [
                xs[(m + 1) % 3] * table[(m + 2) % 3 : (m + 2) % 3 + 1]
                - xs[(m + 2) % 3] * table[(m + 1) % 3 : (m + 1) % 3 + 1]
                - table[3 + m : 4 + m]
                for m in range(3)
            ]

        finished = cross(swirl)
        along = [cross(xs[n] * moment[0] - moment[1 + n]) for n in range(3)]
        for m in range(3):
            for n in range(3):
                term = -3.0 * along[n][m]
                if m != n:
                    other = 3 - m - n
                    part = swirl[other : other + 1]
                    term = term + part if (n - m) % 3 == 1 else term - part
                finished.append(term)
        zero = jnp.zeros((4, LANES), jnp.float32)
        packed = jnp.concatenate(finished + [zero], axis=0) * (alive * scale)
        for h in range(2):
            half = packed[h * SUB : (h + 1) * SUB]
            swapped = jnp.zeros((SUB, LANES), jnp.float32)
            for d in range(SUB):
                moved = half if d == 0 else pltpu.roll(half, d * held, 1)
                moved = jnp.where(group == sub, moved, 0.0)
                swapped = swapped + (moved if d == 0 else pltpu.roll(moved, SUB - d, 0))
            for j in range(SUB):
                parcel[i * SUB + j, :, h * LANES : (h + 1) * LANES] = swapped[j : j + 1]

    def send(there, other):
        pltpu.make_async_remote_copy(
            src_ref=parcel.at[other], dst_ref=inbox.at[me],
            send_sem=parcel_send, recv_sem=parcel_recv, device_id=there, device_id_type=MESH,
        ).start()

    each_other(send)
    keep = pltpu.make_async_copy(parcel.at[me], inbox.at[me], own)
    keep.start()
    keep.wait()
    for sem in (parcel_recv, parcel_send):
        pltpu.make_async_copy(
            inbox.at[pl.ds(0, total - 1)], inbox.at[pl.ds(0, total - 1)], sem
        ).wait()
    pltpu.make_async_copy(
        notes.at[pl.ds(0, total - 1)], notes.at[pl.ds(0, total - 1)], note_send
    ).wait()


def gather_kernel(inbox, vel_ref, grad_ref, final):
    total = inbox.shape[0]
    cells, slots = grad_ref.shape[:2]
    held = cells * slots
    parts = [inbox[other] for other in range(total)]
    while len(parts) > 1:
        parts = [a + b for a, b in zip(parts[0::2], parts[1::2])] + parts[len(parts) // 2 * 2 :]
    result = parts[0]
    for o in range(3):
        for s in range(slots):
            low = o * held + s * cells
            vel_ref[o, s : s + 1, :] = result[:, low : low + cells]
    final[...] = jnp.zeros_like(final)
    for h in range(2):
        final[h : h + 1, :] = result[:, h * LANES : (h + 1) * LANES]
    ends = final[...].T
    lane = lax.broadcasted_iota(jnp.int32, (cells, LANES), 1)
    for s in range(slots):
        table = jnp.zeros((cells, LANES), jnp.float32)
        for o in range(3, 12):
            low = (o % SUB) * held + s * cells
            column = ends[low : low + cells, o // SUB : o // SUB + 1]
            table = jnp.where(lane == o - 3, jnp.broadcast_to(column, (cells, LANES)), table)
        for c in range(cells):
            grad_ref[c, s : s + 1, :] = table[c : c + 1, 0:9]


def per_device(band_cells, cell_counts, cell_assign, wake_pos, wake_strength, wake_core):
    grid_rows = lax.axis_size("row")
    grid_cols = lax.axis_size("col")
    total = grid_rows * grid_cols
    cells, slots = band_cells.shape[1:]
    span = wake_pos.shape[1]
    width = -(-4 * cells * grid_cols // LANES) * LANES
    targets = total * cells * slots
    f32 = jnp.float32
    vmem = pl.BlockSpec(memory_space=pltpu.VMEM)
    hbm = pl.BlockSpec(memory_space=pltpu.HBM)
    bf16 = jnp.bfloat16
    i32 = jnp.int32
    inbox = pl.pallas_call(
        functools.partial(kernel, grid_rows, grid_cols),
        out_shape=jax.ShapeDtypeStruct((total, 1, 2 * LANES), f32),
        in_specs=[hbm] * 6,
        out_specs=hbm,
        scratch_shapes=[
            pltpu.SMEM((3, slots, cells), f32),
            pltpu.SMEM((cells,), i32),
            pltpu.SMEM((cells,), i32),
            pltpu.VMEM((3, span), f32),
            pltpu.VMEM((3, span), f32),
            pltpu.VMEM((1, span), f32),
            pltpu.SemaphoreType.DMA((6,)),
            pltpu.VMEM((ROWS, 2 * CHUNK), bf16),
            pltpu.VMEM((ROWS, 2 * CHUNK), bf16),
            pltpu.VMEM((1, 1, slots * width), f32),
            pltpu.VMEM((total, 1, slots * width), f32),
            pltpu.VMEM((LANES, width), f32),
            pltpu.VMEM((4, targets, LANES), f32),
            pltpu.VMEM((targets, LANES), bf16),
            pltpu.VMEM((DEPTH, span), bf16),
            pltpu.VMEM((LANES, span), jnp.bfloat16),
            pltpu.VMEM((targets, LANES), f32),
            pltpu.VMEM((total, 1, 2 * LANES), f32),
            pltpu.SemaphoreType.DMA,
            pltpu.SemaphoreType.DMA,
            pltpu.SemaphoreType.DMA,
            pltpu.SemaphoreType.DMA,
            pltpu.SemaphoreType.DMA,
        ],
        compiler_params=pltpu.CompilerParams(
            collective_id=0, has_side_effects=True, vmem_limit_bytes=60 * 1024 * 1024
        ),
        name="wake_sums",
    )(band_cells.transpose(0, 2, 1), cell_counts, cell_assign, wake_pos, wake_strength, wake_core)
    velocity, gradient = pl.pallas_call(
        gather_kernel,
        out_shape=(
            jax.ShapeDtypeStruct((3, slots, cells), f32),
            jax.ShapeDtypeStruct((cells, slots, 9), f32),
        ),
        in_specs=[vmem],
        out_specs=(vmem, vmem),
        scratch_shapes=[pltpu.VMEM((LANES, LANES), f32)],
        name="last_sum",
    )(inbox)
    return velocity.transpose(0, 2, 1), gradient.transpose(2, 0, 1)


def solution(mesh):
    placed = (
        P(None, ("row", "col"), None),
        P(("row", "col")),
        P(("row", "col")),
        P(None, ("row", "col")),
        P(None, ("row", "col")),
        P(None, ("row", "col")),
    )
    return jax.shard_map(
        per_device,
        mesh=mesh,
        in_specs=placed,
        out_specs=(P(None, ("row", "col"), None), P(None, ("row", "col"), None)),
        check_vma=False,
    )
```

```python
import functools
import math

import jax
import jax.numpy as jnp
from jax import lax
from jax.experimental import pallas as pl
from jax.experimental.pallas import tpu as pltpu
from jax.sharding import PartitionSpec as P

MESH = pl.DeviceIdType.MESH
LANES = 128
SUB = 8
CHUNK = 1024
PREPARE = 1024
ROWS = 512
STRIP = 32
DEPTH = 48
CENTRE = 0.5


def split_three(value):
    high = value.astype(jnp.bfloat16).astype(jnp.float32)
    rest = value - high
    middle = rest.astype(jnp.bfloat16).astype(jnp.float32)
    return high, middle, rest - middle


def kernel(
    grid_rows, grid_cols,
    band_hbm, counts_hbm, assign_hbm, pos_hbm, str_hbm, core_hbm,
    inbox,
    band_ref, counts_ref, assign_ref, pos_ref, str_ref, core_ref, fetch,
    even, odd, note, notes, turned, place, left, source, weights, sums, parcel, own,
    note_send, note_recv, parcel_send, parcel_recv,
):
    total = grid_rows * grid_cols
    slots, cells = band_ref.shape[1:]
    block = cells * grid_cols
    width = note.shape[2] // slots
    held = cells * slots
    targets = total * held
    me_row = lax.axis_index("row")
    me_col = lax.axis_index("col")
    me = me_row * grid_cols + me_col

    fetches = [
        pltpu.make_async_copy(far, near, fetch.at[i])
        for i, (far, near) in enumerate(
            [
                (assign_hbm, assign_ref), (band_hbm, band_ref), (counts_hbm, counts_ref),
                (pos_hbm, pos_ref), (str_hbm, str_ref), (core_hbm, core_ref),
            ]
        )
    ]
    for one in fetches:
        one.start()

    def each_other(act):
        others = [lax.rem(me_col + z, grid_cols) for z in range(grid_cols)]
        for z in range(1, grid_cols):
            act((me_row, others[z]), me_row * grid_cols + others[z])

        def in_row(step, unused):
            there = lax.rem(me_row + step, grid_rows)
            for z in range(grid_cols):
                act((there, others[z]), there * grid_cols + others[z])
            return unused

        lax.fori_loop(1, grid_rows, in_row, 0)

    barrier = pltpu.get_barrier_semaphore()

    def greet(there, other):
        pl.semaphore_signal(barrier, inc=1, device_id=there, device_id_type=MESH)

    each_other(greet)

    for one in fetches[:3]:
        one.wait()
    lane = lax.broadcasted_iota(jnp.int32, (cells, width), 1)
    row = lax.broadcasted_iota(jnp.int32, (cells, width), 0)
    position = jnp.zeros((cells, width), jnp.int32)
    live = jnp.zeros((cells, width), jnp.float32)
    columns = [[jnp.zeros((cells, width), jnp.float32)] * slots for k in range(3)]
    for t in range(cells):
        for k in range(3):
            for s in range(slots):
                columns[k][s] = jnp.where(row == t, band_ref[k, s, t], columns[k][s])
        position = jnp.where(row == t, lax.rem(assign_ref[t], block), position)
        live = jnp.where(row == t, counts_ref[t].astype(jnp.float32), live)
    chosen = lax.rem(lane, block) == position
    kind = lane // block
    for s in range(slots):
        value = jnp.where(kind == 3, live, 0.0)
        for k in range(3):
            value = jnp.where(kind == k, columns[k][s] - CENTRE, value)
        value = jnp.where(chosen, value, 0.0)
        note[0, :, s * width : (s + 1) * width] = jnp.sum(value, axis=0, keepdims=True)

    for one in fetches[3:]:
        one.wait()
    span = source.shape[1]

    def prepare(index, unused):
        cols = pl.ds(pl.multiple_of(index * PREPARE, PREPARE), PREPARE)
        ys = [pos_ref[k : k + 1, cols] - CENTRE for k in range(3)]
        al = [str_ref[k : k + 1, cols] for k in range(3)]
        core = core_ref[0:1, cols]
        core_sq = core * core
        norm = ys[0] * ys[0] + ys[1] * ys[1] + ys[2] * ys[2] + core_sq
        be = [
            ys[(m + 1) % 3] * al[(m + 2) % 3] - ys[(m + 2) % 3] * al[(m + 1) % 3]
            for m in range(3)
        ]
        ones = jnp.ones((1, PREPARE), jnp.float32)
        blank = jnp.zeros((3, PREPARE), jnp.float32)
        one, two, three = split_three(jnp.concatenate(ys + [norm, ones, blank], axis=0))
        source[:, cols] = jnp.concatenate([one, one, one, two, two, three], axis=0).astype(
            jnp.bfloat16
        )
        pad = jnp.zeros((2, PREPARE), jnp.float32)
        base = jnp.concatenate(al + be + [pad], axis=0)
        split = [split_three(base)] + [split_three(base * g) for g in ys + [norm]]
        rows = [split[b][j] for j in range(3) for b in range(5)]
        rows.append(jnp.zeros((SUB, PREPARE), jnp.float32))
        weights[:, cols] = jnp.concatenate(rows, axis=0).astype(jnp.bfloat16)
        return unused

    ahead = span // PREPARE // 2
    lax.fori_loop(0, ahead, prepare, 0)

    pl.semaphore_wait(barrier, total - 1)

    def tell(there, other):
        pltpu.make_async_remote_copy(
            src_ref=note.at[0], dst_ref=notes.at[me], send_sem=note_send, recv_sem=note_recv,
            device_id=there, device_id_type=MESH,
        ).start()

    each_other(tell)
    notes[me] = note[0]

    lax.fori_loop(ahead, span // PREPARE, prepare, 0)

    pltpu.make_async_copy(
        notes.at[pl.ds(0, total - 1)], notes.at[pl.ds(0, total - 1)], note_recv
    ).wait()
    turned[...] = jnp.zeros_like(turned)
    for g in range(grid_rows):
        merged = notes[g * grid_cols]
        for z in range(1, grid_cols):
            merged = merged + notes[g * grid_cols + z]
        for s in range(slots):
            turned[g * slots + s : g * slots + s + 1, :] = merged[:, s * width : (s + 1) * width]
    columns = jnp.concatenate(
        [turned[:, w : w + LANES].T for w in range(0, width, LANES)], axis=0
    )
    for g in range(grid_rows):
        for z in range(grid_cols):
            for s in range(slots):
                at = ((g * grid_cols + z) * slots + s) * cells
                for k in range(4):
                    low = k * block + z * cells
                    column = columns[low : low + cells, g * slots + s : g * slots + s + 1]
                    wide = jnp.broadcast_to(column, (cells, LANES))
                    if k == 3:
                        wide = jnp.where(wide > s + 0.5, 1.0, 0.0)
                    place[k, at : at + cells, :] = wide

    def sides(index, unused):
        rows = pl.ds(pl.multiple_of(index * LANES, LANES), LANES)
        lane = lax.broadcasted_iota(jnp.int32, (LANES, LANES), 1)
        xs = [place[k, rows, :] for k in range(3)]
        value = jnp.where(lane % SUB == 3, 1.0, 0.0)
        value = jnp.where(
            lane % SUB == 4, xs[0] * xs[0] + xs[1] * xs[1] + xs[2] * xs[2], value
        )
        for k in range(3):
            value = jnp.where(lane % SUB == k, -2.0 * xs[k], value)
        one, two, three = split_three(value)
        part = lane // SUB
        value = jnp.where((part == 1) | (part == 4), two, jnp.where(part == 2, three, one))
        left[rows, :] = jnp.where(part < 6, value, 0.0).astype(jnp.bfloat16)
        return unused

    lax.fori_loop(0, targets // LANES, sides, 0)

    sums[...] = jnp.zeros_like(sums)

    parts = targets // ROWS
    steps = (span // CHUNK) * parts

    def where_at(index):
        cols = pl.ds(pl.multiple_of((index // parts) * CHUNK, CHUNK), CHUNK)
        first = lax.rem(index, parts) * ROWS
        return cols, first

    def radii(index):
        cols, first = where_at(index)

        rows = pl.ds(pl.multiple_of(first, ROWS), ROWS)
        return jnp.dot(
            left[rows, 0:DEPTH], source[:, cols], preferred_element_type=jnp.float32
        )

    def powers(radius, store):
        for low in range(0, ROWS, STRIP):
            inverse = lax.rsqrt(radius[low : low + STRIP])
            square = inverse * inverse
            power = square * square * inverse
            high = power.astype(jnp.bfloat16)
            rest = (power - high.astype(jnp.float32)).astype(jnp.bfloat16)
            store[low : low + STRIP, 0:CHUNK] = high
            store[low : low + STRIP, CHUNK : 2 * CHUNK] = rest

    def add(index, store):
        cols, first = where_at(index)
        rows = pl.ds(pl.multiple_of(first, ROWS), ROWS)
        both = jnp.concatenate([weights[:, cols]] * 2, axis=1)
        sums[rows, :] += lax.dot_general(
            store[...], both, (((1,), (1,)), ((), ())), preferred_element_type=jnp.float32
        )

    powers(radii(0), even)

    def pairs(count, unused):
        index = 2 * count
        radius = radii(index + 1)
        add(index, even)
        powers(radius, odd)
        radius = radii(index + 2)
        add(index + 1, odd)
        powers(radius, even)
        return unused

    lax.fori_loop(0, steps // 2 - 1, pairs, 0)
    radius = radii(steps - 1)
    add(steps - 2, even)
    powers(radius, odd)
    add(steps - 1, odd)

    scale = -1.0 / (4.0 * math.pi)
    lane = lax.broadcasted_iota(jnp.int32, (LANES, LANES), 1)
    sub = lax.broadcasted_iota(jnp.int32, (SUB, LANES), 0)
    group = lax.broadcasted_iota(jnp.int32, (SUB, LANES), 1) // held
    for i in range(targets // LANES):
        rows = slice(i * LANES, (i + 1) * LANES)
        tile = sums[rows, :]
        for k in range(4):
            tile = jnp.where(lane == 120 + k, place[k, rows, :], tile)
        tile = tile.T
        moment = [
            tile[b * SUB : (b + 1) * SUB]
            + (tile[40 + b * SUB : 48 + b * SUB] + tile[80 + b * SUB : 88 + b * SUB])
            for b in range(5)
        ]
        xs = [tile[120 + k : 121 + k] for k in range(3)]
        alive = tile[123:124]
        norm = xs[0] * xs[0] + xs[1] * xs[1] + xs[2] * xs[2]
        swirl = norm * moment[0] + moment[4]
        for n in range(3):
            swirl = swirl - (2.0 * xs[n]) * moment[1 + n]

        def cross(table):
            return [
                xs[(m + 1) % 3] * table[(m + 2) % 3 : (m + 2) % 3 + 1]
                - xs[(m + 2) % 3] * table[(m + 1) % 3 : (m + 1) % 3 + 1]
                - table[3 + m : 4 + m]
                for m in range(3)
            ]

        finished = cross(swirl)
        along = [cross(xs[n] * moment[0] - moment[1 + n]) for n in range(3)]
        for m in range(3):
            for n in range(3):
                term = -3.0 * along[n][m]
                if m != n:
                    other = 3 - m - n
                    part = swirl[other : other + 1]
                    term = term + part if (n - m) % 3 == 1 else term - part
                finished.append(term)
        zero = jnp.zeros((4, LANES), jnp.float32)
        packed = jnp.concatenate(finished + [zero], axis=0) * (alive * scale)
        for h in range(2):
            half = packed[h * SUB : (h + 1) * SUB]
            swapped = jnp.zeros((SUB, LANES), jnp.float32)
            for d in range(SUB):
                moved = half if d == 0 else pltpu.roll(half, d * held, 1)
                moved = jnp.where(group == sub, moved, 0.0)
                swapped = swapped + (moved if d == 0 else pltpu.roll(moved, SUB - d, 0))
            for j in range(SUB):
                parcel[i * SUB + j, :, h * LANES : (h + 1) * LANES] = swapped[j : j + 1]

    def send(there, other):
        pltpu.make_async_remote_copy(
            src_ref=parcel.at[other], dst_ref=inbox.at[me],
            send_sem=parcel_send, recv_sem=parcel_recv, device_id=there, device_id_type=MESH,
        ).start()

    each_other(send)
    keep = pltpu.make_async_copy(parcel.at[me], inbox.at[me], own)
    keep.start()
    keep.wait()
    for sem in (parcel_recv, parcel_send):
        pltpu.make_async_copy(
            inbox.at[pl.ds(0, total - 1)], inbox.at[pl.ds(0, total - 1)], sem
        ).wait()
    pltpu.make_async_copy(
        notes.at[pl.ds(0, total - 1)], notes.at[pl.ds(0, total - 1)], note_send
    ).wait()


def gather_kernel(inbox, vel_ref, grad_ref, final):
    total = inbox.shape[0]
    cells, slots = grad_ref.shape[:2]
    held = cells * slots
    parts = [inbox[other] for other in range(total)]
    while len(parts) > 1:
        parts = [a + b for a, b in zip(parts[0::2], parts[1::2])] + parts[len(parts) // 2 * 2 :]
    result = parts[0]
    for o in range(3):
        for s in range(slots):
            low = o * held + s * cells
            vel_ref[o, s : s + 1, :] = result[:, low : low + cells]
    final[...] = jnp.zeros_like(final)
    for h in range(2):
        final[h : h + 1, :] = result[:, h * LANES : (h + 1) * LANES]
    ends = final[...].T
    lane = lax.broadcasted_iota(jnp.int32, (cells, LANES), 1)
    for s in range(slots):
        table = jnp.zeros((cells, LANES), jnp.float32)
        for o in range(3, 12):
            low = (o % SUB) * held + s * cells
            column = ends[low : low + cells, o // SUB : o // SUB + 1]
            table = jnp.where(lane == o - 3, jnp.broadcast_to(column, (cells, LANES)), table)
        for c in range(cells):
            grad_ref[c, s : s + 1, :] = table[c : c + 1, 0:9]


def per_device(band_cells, cell_counts, cell_assign, wake_pos, wake_strength, wake_core):
    grid_rows = lax.axis_size("row")
    grid_cols = lax.axis_size("col")
    total = grid_rows * grid_cols
    cells, slots = band_cells.shape[1:]
    span = wake_pos.shape[1]
    width = -(-4 * cells * grid_cols // LANES) * LANES
    targets = total * cells * slots
    f32 = jnp.float32
    vmem = pl.BlockSpec(memory_space=pltpu.VMEM)
    hbm = pl.BlockSpec(memory_space=pltpu.HBM)
    bf16 = jnp.bfloat16
    i32 = jnp.int32
    inbox = pl.pallas_call(
        functools.partial(kernel, grid_rows, grid_cols),
        out_shape=jax.ShapeDtypeStruct((total, 1, 2 * LANES), f32),
        in_specs=[hbm] * 6,
        out_specs=hbm,
        scratch_shapes=[
            pltpu.SMEM((3, slots, cells), f32),
            pltpu.SMEM((cells,), i32),
            pltpu.SMEM((cells,), i32),
            pltpu.VMEM((3, span), f32),
            pltpu.VMEM((3, span), f32),
            pltpu.VMEM((1, span), f32),
            pltpu.SemaphoreType.DMA((6,)),
            pltpu.VMEM((ROWS, 2 * CHUNK), bf16),
            pltpu.VMEM((ROWS, 2 * CHUNK), bf16),
            pltpu.VMEM((1, 1, slots * width), f32),
            pltpu.VMEM((total, 1, slots * width), f32),
            pltpu.VMEM((LANES, width), f32),
            pltpu.VMEM((4, targets, LANES), f32),
            pltpu.VMEM((targets, LANES), bf16),
            pltpu.VMEM((DEPTH, span), bf16),
            pltpu.VMEM((LANES, span), jnp.bfloat16),
            pltpu.VMEM((targets, LANES), f32),
            pltpu.VMEM((total, 1, 2 * LANES), f32),
            pltpu.SemaphoreType.DMA,
            pltpu.SemaphoreType.DMA,
            pltpu.SemaphoreType.DMA,
            pltpu.SemaphoreType.DMA,
            pltpu.SemaphoreType.DMA,
        ],
        compiler_params=pltpu.CompilerParams(
            collective_id=0, has_side_effects=True, vmem_limit_bytes=60 * 1024 * 1024
        ),
        name="wake_sums",
    )(band_cells.transpose(0, 2, 1), cell_counts, cell_assign, wake_pos, wake_strength, wake_core)
    velocity, gradient = pl.pallas_call(
        gather_kernel,
        out_shape=(
            jax.ShapeDtypeStruct((3, slots, cells), f32),
            jax.ShapeDtypeStruct((cells, slots, 9), f32),
        ),
        in_specs=[vmem],
        out_specs=(vmem, vmem),
        scratch_shapes=[pltpu.VMEM((LANES, LANES), f32)],
        name="last_sum",
    )(inbox)
    return velocity.transpose(0, 2, 1), gradient.transpose(2, 0, 1)


def solution(mesh):
    placed = (
        P(None, ("row", "col"), None),
        P(("row", "col")),
        P(("row", "col")),
        P(None, ("row", "col")),
        P(None, ("row", "col")),
        P(None, ("row", "col")),
    )
    return jax.shard_map(
        per_device,
        mesh=mesh,
        in_specs=placed,
        out_specs=(P(None, ("row", "col"), None), P(None, ("row", "col"), None)),
        check_vma=False,
    )
```
